256 devices in a mesh: path: 32 (over z_hi, y, core), fsdp: 8 (over z_lo, x).
Axes of the slice: x: 4, y: 4, z: 8 (z_hi: 4, z_lo: 2; z = z_hi * 2 + z_lo), core: 2. Of those that a mesh axis runs over, the one named last changes fastest.
Arguments:
- inputs: bfloat16 [32, 6144, 2048], P('path', 'fsdp'), may hold values from -6 to 6
- targets: bfloat16 [32, 6144, 2048], P('path', 'fsdp'), may hold values from -6 to 6
- token_ids: int32 [32, 6144], P('path', 'fsdp'), may hold values from 0 to 31999, as said below
- path_weights: bfloat16 [32, 2048, 2048], P('path', 'fsdp'), may hold values from -6 to 6
- stale_deltas: bfloat16 [32, 2048, 2048], P('path', 'fsdp'), may hold values from -6 to 6
- module_params: float32 [4, 2048, 2048], P(None, 'fsdp', 'path'), may hold values from -6 to 6
- momentum: float32 [4, 2048, 2048], P(None, 'fsdp', 'path'), may hold values from -3 to 3
- module_of_path: int32 [32], replicated, may hold values from 0 to 3, as said below
- sharing_counts: int32 [4], replicated, may hold values from 1 to 16, as said below
Outputs:
- next_weights: bfloat16 [32, 2048, 2048], P('path', 'fsdp')
- new_params: float32 [4, 2048, 2048], P(None, 'fsdp', 'path')
- new_momentum: float32 [4, 2048, 2048], P(None, 'fsdp', 'path')
The draws below stay inside these ranges and needn't reach their ends.
Inputs may be any that keep to these rules, and one draw needn't show every extreme that they name: `module_of_path`: every module is used by at least one path; one module is used by exactly 16 paths, every other by fewer. sharing_counts[m] is the number of paths p with module_of_path[p] = m. `token_ids`: each path's tokens with id 0 form a suffix that leaves at least a quarter of its 6144 tokens real.
All inputs are finite; a program needn't handle non-finite values.
Results may differ from the reference program's by a relative error of at most 0.015.
Values may be sent and summed in bfloat16 or wider, within the bound.
No kernel may reach another device: no remote copies, remote signals or barrier semaphores. Data moves between devices by JAX's collectives and lax.ppermute only.
A program may use at most 128 MiB of HBM per device.

```python
import math
import jax
import jax.numpy as jnp
from jax import lax

DI = 2048
DO = 2048
MODULES = 4
VOCAB = 32000
TOK_DEV = 768
PATHS = 32
TOK_PATH = 6144
N_FSDP = 8


def incidence(key):
    fill_key, relabel_key, order_key = jax.random.split(key, 3)
    places = jnp.arange(PATHS, dtype=jnp.int32)
    half = PATHS // 2
    others = jax.random.randint(fill_key, (PATHS,), 1, MODULES).astype(jnp.int32)
    fixed = places - half + 1
    picked = jnp.where(places < half, 0, jnp.where(places < half + MODULES - 1, fixed, others))
    relabel = jax.random.permutation(relabel_key, MODULES)
    picked = relabel[picked]
    order = jax.random.permutation(order_key, PATHS)
    return picked[order].astype(jnp.int32)


def draw_module_of_path(key, part):
    return incidence(key)


def draw_sharing_counts(key, part):
    chosen = incidence(key)
    hits = (chosen[:, None] == jnp.arange(MODULES, dtype=jnp.int32)[None, :]).astype(jnp.int32)
    return jnp.sum(hits, axis=0).astype(jnp.int32)


def draw_token_ids(key, part):
    key = jax.random.fold_in(key, 7)
    length_key, id_key = jax.random.split(key)
    lengths = jax.random.randint(length_key, (PATHS, 1), TOK_PATH // 4 + 1, TOK_PATH + 1)
    values = jax.random.randint(id_key, (PATHS, TOK_PATH), 1, VOCAB)
    places = jnp.arange(TOK_PATH, dtype=jnp.int32)[None, :]
    return jnp.where(places < lengths, values, 0).astype(jnp.int32)


def block_levels(rng, shape, pieces, low, high):
    level, own = 1.0, jax.random.fold_in(rng, 6)
    for axis_at, blocks in pieces:
        steps = jnp.exp(jax.random.uniform(jax.random.fold_in(own, axis_at), (blocks,), jnp.float32, low / len(pieces), high / len(pieces)))
        level = level * jnp.repeat(steps, shape[axis_at] // blocks).reshape([-1 if axis == axis_at else 1 for axis in range(len(shape))])
    return level


def gaussian(rng, extent, scale, most, cuts=(), held_as=jnp.bfloat16):
    entries = scale * jax.random.normal(rng, extent, jnp.float32)
    if cuts:
        entries = entries * block_levels(rng, extent, cuts, -0.22, 0.18)
    return jnp.clip(entries, -most, most).astype(held_as)


def setup_inputs(seed: int = 0) -> dict:
    key_of = jax.random.split(jax.random.key(seed), 10)
    return {
        "inputs": gaussian(key_of[0], (PATHS, TOK_PATH, DI), 1.0, 6.0, ((0, 32), (1, 8))),
        "targets": gaussian(key_of[1], (PATHS, TOK_PATH, DO), 1.0, 6.0, ((0, 32), (1, 8))),
        "token_ids": draw_token_ids(jax.random.fold_in(key_of[9], 71), 0),
        "path_weights": gaussian(key_of[3], (PATHS, DI, DO), 1.0, 6.0, ((0, 32), (1, 8))),
        "stale_deltas": gaussian(key_of[4], (PATHS, DI, DO), 1.0, 6.0, ((0, 32), (1, 8))),
        "module_params": gaussian(key_of[5], (MODULES, DI, DO), 1.0, 6.0, ((1, 8), (2, 32)), jnp.float32),
        "momentum": gaussian(key_of[6], (MODULES, DI, DO), 0.5, 3.0, ((1, 8), (2, 32)), jnp.float32),
        "module_of_path": draw_module_of_path(jax.random.fold_in(key_of[9], 71), 0),
        "sharing_counts": draw_sharing_counts(jax.random.fold_in(key_of[9], 71), 0),
    }


def reference(inputs, targets, token_ids, path_weights, stale_deltas, module_params, momentum, module_of_path, sharing_counts):
    table = (module_of_path[:, None] == jnp.arange(MODULES, dtype=jnp.int32)[None, :]).astype(jnp.float32)

    def accumulate(total, items):
        row, delta = items
        return (total + row[:, None, None] * delta.astype(jnp.float32)[None], None)
    total, unused = lax.scan(accumulate, jnp.zeros((MODULES, DI, DO), jnp.float32), (table, stale_deltas))
    outer_grad = total / sharing_counts.astype(jnp.float32)[:, None, None]
    new_momentum = 0.9 * momentum + outer_grad
    outer_step = 0.7 * (outer_grad + 0.9 * new_momentum)
    new_params = module_params - outer_step
    outer_step_b = lax.optimization_barrier(outer_step.astype(jnp.bfloat16))

    def one_path(items):
        block_in, block_target, block_ids, weights, module = items
        values = block_in.astype(jnp.float32)
        scale = lax.rsqrt(lax.optimization_barrier(jnp.mean(values * values, axis=-1, keepdims=True)) + 1e-06)
        normed = (values * scale).astype(jnp.bfloat16)
        mask = (block_ids != 0).astype(jnp.float32)
        count = jnp.sum(mask)
        projected = jnp.dot(normed, weights, preferred_element_type=jnp.float32) / math.sqrt(DI)
        residual_rows = ((projected - block_target.astype(jnp.float32)) * mask[:, None]).astype(jnp.bfloat16)
        grad = jnp.zeros((DI, DO), jnp.float32)
        for block in range(N_FSDP):
            lower = block * TOK_DEV
            part = jnp.dot(normed[lower:lower + TOK_DEV].T, residual_rows[lower:lower + TOK_DEV], preferred_element_type=jnp.float32)
            part = lax.optimization_barrier(part.astype(jnp.bfloat16))
            grad = grad + part.astype(jnp.float32)
        grad = grad / jnp.sqrt(count)
        correction = outer_step_b[module].astype(jnp.float32)
        return (weights.astype(jnp.float32) - 0.25 * grad - correction).astype(jnp.bfloat16)
    next_weights = lax.map(one_path, (inputs, targets, token_ids, path_weights, module_of_path))
    return (next_weights, new_params, new_momentum)
```

```python
import functools
import math

import jax
import jax.numpy as jnp
from jax import lax
from jax.experimental import pallas as pl
from jax.experimental.pallas import tpu as pltpu
from jax.sharding import PartitionSpec as P

Z_HI, Y, CORES, Z_LO, X = 4, 4, 2, 2, 4
HALF = 64
TILE = 512
BASE = 32.0
EXTRA = 16
VMEM_LIMIT = 48 * 1024 * 1024
SMALL_LIMIT = 16 * 1024 * 1024


def ring(step):
    return [(z * X + x, z * X + (x + step) % X) for z in range(Z_LO) for x in range(X)]


def pair():
    return [(z * X + x, (1 - z) * X + x) for z in range(Z_LO) for x in range(X)]


def along_y(step):
    return [
        ((z * Y + y) * CORES + c, (z * Y + (y + step) % Y) * CORES + c)
        for z in range(Z_HI)
        for y in range(Y)
        for c in range(CORES)
    ]


def cores():
    return [(p, p ^ 1) for p in range(Z_HI * Y * CORES)]


def owner(place, k):
    own_z, own_x = place // X, place % X
    return ((own_z + k // X) % Z_LO) * X + (own_x + k % X) % X


def norm_kernel(place_ref, x_ref, n_ref):
    values = x_ref[...].astype(jnp.float32)
    scale = lax.rsqrt(jnp.mean(values * values, axis=-1, keepdims=True) + 1e-06)
    width = x_ref.shape[1] // (Z_LO * X)
    for k in range(Z_LO * X):
        start = pl.multiple_of(owner(place_ref[1], k) * width, width)
        block = x_ref[:, pl.ds(start, width)].astype(jnp.float32) * scale
        n_ref[:, k * width : (k + 1) * width] = block.astype(jnp.bfloat16)


def norm(place, x):
    rows, width = x.shape
    step = 128
    block = pl.BlockSpec((step, width), lambda i, s: (i, 0))
    return pl.pallas_call(
        norm_kernel,
        grid_spec=pltpu.PrefetchScalarGridSpec(
            num_scalar_prefetch=1, grid=(rows // step,), in_specs=[block], out_specs=block
        ),
        out_shape=jax.ShapeDtypeStruct((rows, width), jnp.bfloat16),
        compiler_params=pltpu.CompilerParams(vmem_limit_bytes=SMALL_LIMIT),
        cost_estimate=pl.CostEstimate(flops=3 * rows * width, bytes_accessed=4 * rows * width, transcendentals=rows),
        name="norm",
    )(place, x)


def grad_kernel(n_ref, target_ref, mask_ref, *rest):
    pieces, outs, w_ref = rest[:8], rest[-9:-1], rest[-1]
    depth = pieces[0].shape[0]
    for k, piece in enumerate(pieces):
        w_ref[k * depth : (k + 1) * depth, :] = piece[...]
    projected = jnp.dot(n_ref[...], w_ref[...], preferred_element_type=jnp.float32)
    projected = projected * (1.0 / math.sqrt(n_ref.shape[1]))
    rows = ((projected - target_ref[...].astype(jnp.float32)) * mask_ref[...]).astype(jnp.bfloat16)
    for k, out in enumerate(outs):
        out[:depth, :] = lax.dot_general(
            n_ref[:, k * depth : (k + 1) * depth],
            rows,
            (((0,), (0,)), ((), ())),
            preferred_element_type=jnp.float32,
        ).astype(jnp.bfloat16)
    more = outs[0].shape[0] - depth
    if more:
        count = jnp.sum(mask_ref[...])
        high = jnp.floor(count * (1.0 / BASE))
        low = count - BASE * high
        upper = lax.broadcasted_iota(jnp.int32, (more, TILE), 0) < more // 2
        for out in outs:
            out[depth:, :] = jnp.where(upper, high, low).astype(jnp.bfloat16)


def grads(normed, targets, mask, weights, pieces, chunk, width, more, deps=()):
    rows, features = normed.shape
    depth = weights.shape[0]
    steps = width // TILE
    base = chunk * steps
    piece = pl.BlockSpec((depth, TILE), lambda j: (0, j))
    out = pl.BlockSpec((depth + more, TILE), lambda j: (0, j))
    return pl.pallas_call(
        grad_kernel,
        grid=(steps,),
        in_specs=[
            pl.BlockSpec((rows, features), lambda j: (0, 0), pipeline_mode=pl.Buffered(1)),
            pl.BlockSpec((rows, TILE), lambda j: (0, base + j)),
            pl.BlockSpec((rows, 1), lambda j: (0, 0), pipeline_mode=pl.Buffered(1)),
            pl.BlockSpec((depth, TILE), lambda j: (0, base + j)),
        ]
        + [piece] * 7
        + [pl.BlockSpec(memory_space=pl.ANY)] * len(deps),
        out_specs=[out] * 8,
        out_shape=[jax.ShapeDtypeStruct((depth + more, width), jnp.bfloat16)] * 8,
        scratch_shapes=[pltpu.VMEM((features, TILE), jnp.bfloat16)],
        compiler_params=pltpu.CompilerParams(vmem_limit_bytes=VMEM_LIMIT),
        cost_estimate=pl.CostEstimate(
            flops=4 * rows * features * width,
            bytes_accessed=2 * rows * features + 4 * features * width + 2 * rows * width,
            transcendentals=0,
        ),
        name="grads",
    )(normed, targets, mask, weights, *pieces, *deps)


def deal_kernel(place_ref, *refs):
    for source, out in zip(refs[:Y], refs[Y:]):
        out[0] = source[...]


def deal(place, delta):
    rows = delta.shape[0]
    lanes = CORES * HALF

    def at(step):
        return lambda z, s: (0, z * Y + (s[0] // CORES + step) % Y)

    return pl.pallas_call(
        deal_kernel,
        grid_spec=pltpu.PrefetchScalarGridSpec(
            num_scalar_prefetch=1,
            grid=(Z_HI,),
            in_specs=[pl.BlockSpec((rows, lanes), at(step)) for step in range(Y)],
            out_specs=[pl.BlockSpec((1, rows, lanes), lambda z, s: (z, 0, 0))] * Y,
        ),
        out_shape=[jax.ShapeDtypeStruct((Z_HI, rows, lanes), jnp.bfloat16)] * Y,
        compiler_params=pltpu.CompilerParams(vmem_limit_bytes=SMALL_LIMIT),
        cost_estimate=pl.CostEstimate(flops=0, bytes_accessed=4 * delta.size, transcendentals=0),
        name="deal",
    )(place, *[delta] * Y)


def halves(value):
    rows = value.shape[0] // 2
    top, bottom = value[:rows], value[rows:]
    left = lax.broadcasted_iota(jnp.int32, top.shape, 1) < HALF
    first = jnp.where(left, top, pltpu.roll(bottom, HALF, 1))
    second = jnp.where(left, pltpu.roll(top, HALF, 1), bottom)
    return first, second


def place_kernel(place_ref, module_ref, *refs):
    sources, mine, theirs = refs[:Y], refs[-2], refs[-1]
    path = place_ref[0]
    core, own_y, own_z = path % CORES, (path // CORES) % Y, path // (CORES * Y)
    values = [source[0].astype(jnp.float32) for source in sources]
    labels = [module_ref[(own_z * Y + (own_y + Y - step) % Y) * CORES + core] for step in range(Y)]
    for m in range(mine.shape[1]):
        total = jnp.zeros_like(values[0])
        for value, label in zip(values, labels):
            total = total + jnp.where(label == m, 1.0, 0.0) * value
        first, second = halves(total)
        mine[0, m] = jnp.where(core == 0, first, second).astype(jnp.bfloat16)
        theirs[0, m] = jnp.where(core == 0, second, first).astype(jnp.bfloat16)


def place_sums(place, module_of_path, sources, modules, deps):
    zs, rows, lanes = sources[0].shape

    return pl.pallas_call(
        place_kernel,
        grid_spec=pltpu.PrefetchScalarGridSpec(
            num_scalar_prefetch=2,
            grid=(zs,),
            in_specs=[pl.BlockSpec((1, rows, lanes), lambda z, s, t: (z, 0, 0))] * Y
            + [pl.BlockSpec(memory_space=pl.ANY)] * len(deps),
            out_specs=[pl.BlockSpec((1, modules, rows // 2, lanes), lambda z, s, t: (z, 0, 0, 0))] * 2,
        ),
        out_shape=[jax.ShapeDtypeStruct((zs, modules, rows // 2, lanes), jnp.bfloat16)] * 2,
        compiler_params=pltpu.CompilerParams(vmem_limit_bytes=SMALL_LIMIT),
        cost_estimate=pl.CostEstimate(
            flops=8 * modules * zs * rows * lanes, bytes_accessed=16 * zs * rows * lanes, transcendentals=0
        ),
        name="place_sums",
    )(place, module_of_path, *sources, *deps)


def outer_kernel(sources, count_ref, *refs):
    parts = refs[:sources]
    params_ref, momentum_ref = refs[sources : sources + 2]
    params_out, momentum_out, step_out = refs[-3:]
    count = count_ref[pl.program_id(0)].astype(jnp.float32)
    total = parts[0][0].astype(jnp.float32)
    for part in parts[1:]:
        total = total + part[0].astype(jnp.float32)
    turned = total.T
    total = jnp.concatenate([turned[:HALF], turned[HALF:]], axis=1)
    outer_grad = total / count
    new_momentum = 0.9 * momentum_ref[0] + outer_grad
    step = 0.7 * (outer_grad + 0.9 * new_momentum)
    momentum_out[0] = new_momentum
    params_out[0] = params_ref[0] - step
    rows = step.shape[1] // 2
    step_out[0] = jnp.concatenate([step[:, :rows], step[:, rows:]], axis=0).T.astype(jnp.bfloat16)


def outer(sharing_counts, parts, params, momentum, deps):
    modules, columns, rows = params.shape
    state = pl.BlockSpec((1, columns, rows), lambda m, s: (m, 0, 0))
    packed = pl.BlockSpec((1,) + parts[0].shape[1:], lambda m, s: (m, 0, 0))
    return pl.pallas_call(
        functools.partial(outer_kernel, len(parts)),
        grid_spec=pltpu.PrefetchScalarGridSpec(
            num_scalar_prefetch=1,
            grid=(modules,),
            in_specs=[packed] * len(parts) + [state, state] + [pl.BlockSpec(memory_space=pl.ANY)] * len(deps),
            out_specs=[state, state, packed],
        ),
        out_shape=[
            jax.ShapeDtypeStruct(params.shape, jnp.float32),
            jax.ShapeDtypeStruct(params.shape, jnp.float32),
            jax.ShapeDtypeStruct(parts[0].shape, jnp.bfloat16),
        ],
        compiler_params=pltpu.CompilerParams(vmem_limit_bytes=SMALL_LIMIT),
        cost_estimate=pl.CostEstimate(flops=8 * params.size, bytes_accessed=32 * params.size, transcendentals=0),
        name="outer",
    )(sharing_counts, *parts, params, momentum, *deps)


def final_kernel(terms, first_chunk, place_ref, module_ref, weight_ref, step_ref, *refs):
    depth = weight_ref.shape[0]
    grad = refs[0][...].astype(jnp.float32)
    for term in refs[1:terms]:
        grad = grad + term[...].astype(jnp.float32)
    if first_chunk:
        out, rate_out = refs[-2:]
        half = (grad.shape[0] - depth) // 2
        count = BASE * grad[depth : depth + half, :128] + grad[depth + half :, :128]
        rate_out[...] = 0.25 / jnp.sqrt(count)
        rate, grad = rate_out[0:1, 0:1], grad[:depth]
    else:
        rate, out = refs[terms][0:1, 0:1], refs[-1]
    inner = weight_ref[...].astype(jnp.float32) - rate * grad
    rows = step_ref.shape[2]
    left = lax.broadcasted_iota(jnp.int32, (rows, CORES * HALF), 1) < HALF
    for k in range(step_ref.shape[0] // CORES):
        first = step_ref[CORES * k, 0].astype(jnp.float32)
        second = step_ref[CORES * k + 1, 0].astype(jnp.float32)
        top = jnp.where(left, first, pltpu.roll(second, HALF, 1))
        bottom = jnp.where(left, pltpu.roll(first, HALF, 1), second)
        span = slice(k * CORES * HALF, (k + 1) * CORES * HALF)
        out[:rows, span] = (inner[:rows, span] - top).astype(jnp.bfloat16)
        out[rows:, span] = (inner[rows:, span] - bottom).astype(jnp.bfloat16)


def final(place, module_of_path, weights, steps, terms, earlier, chunk, width):
    depth, features = weights.shape
    grid = width // TILE
    base = chunk * grid
    rows, lanes = steps.shape[2:]
    tiles = TILE // HALF
    first = earlier is None
    rate = pl.BlockSpec((8, 128), lambda j, s, t: (0, 0))
    extra = [] if first else [rate, pl.BlockSpec(memory_space=pl.ANY)]
    out = pl.BlockSpec((depth, TILE), lambda j, s, t: (0, base + j))
    result = jax.ShapeDtypeStruct((depth, features), jnp.bfloat16)
    return pl.pallas_call(
        functools.partial(final_kernel, len(terms), first),
        grid_spec=pltpu.PrefetchScalarGridSpec(
            num_scalar_prefetch=2,
            grid=(grid,),
            in_specs=[
                pl.BlockSpec((depth, TILE), lambda j, s, t: (0, base + j)),
                pl.BlockSpec((tiles, 1, rows, lanes), lambda j, s, t: (base + j, t[s[0]], 0, 0)),
            ]
            + [pl.BlockSpec((terms[0].shape[0], TILE), lambda j, s, t: (0, j))] * len(terms)
            + extra,
            out_specs=[out, rate] if first else out,
        ),
        out_shape=[result, jax.ShapeDtypeStruct((8, 128), jnp.float32)] if first else result,
        input_output_aliases={} if first else {5 + len(terms): 0},
        compiler_params=pltpu.CompilerParams(vmem_limit_bytes=SMALL_LIMIT),
        cost_estimate=pl.CostEstimate(flops=8 * depth * width, bytes_accessed=14 * depth * width, transcendentals=0),
        name="final",
    )(place, module_of_path, weights, steps, *terms, *([] if first else [earlier[1], earlier[0]]))


def after(value, *deps):
    return lax.optimization_barrier((value,) + deps)[0]


def shift(value, way):
    return lax.ppermute(value, "fsdp", way)


def by_offset(s, left, right, far, other, other_left, other_right, other_far):
    pieces = [None] * 8
    pieces[-s % X], pieces[s % X], pieces[2] = left, right, far
    pieces[X], pieces[X + -s % X], pieces[X + s % X], pieces[X + 2] = other, other_left, other_right, other_far
    return pieces[1:]


def gather_first(own):
    up, down, across = ring(1), ring(-1), pair()
    with jax.named_scope("shards"):
        left, right, other = shift(own, up), shift(own, down), shift(own, across)
    begun = (left, right, other)
    with jax.named_scope("shards_on"):
        far = shift(after(left, right, other), up)
        other_right = shift(after(other, left, right), down)
        other_left = shift(after(left, right, other), across)
    with jax.named_scope("shards_last"):
        other_far = shift(after(other_left, far), up)
    return by_offset(1, left, right, far, other, other_left, other_right, other_far), begun, other_left, other_far


def gather_second(own, other_left_a, other_far_a):
    up, down, across = ring(1), ring(-1), pair()
    with jax.named_scope("late_shards"):
        left = shift(own, down)
        other = shift(after(own, other_left_a), across)
        right = shift(after(own, other_far_a), up)
    with jax.named_scope("late_shards_on"):
        far, other_left, other_right = shift(left, down), shift(left, across), shift(other, up)
    with jax.named_scope("late_shards_last"):
        other_far = shift(other_left, down)
    return by_offset(-1, left, right, far, other, other_left, other_right, other_far), (left, other)


def add(*values):
    total = values[0].astype(jnp.float32)
    for value in values[1:]:
        total = total + value.astype(jnp.float32)
    return total.astype(jnp.bfloat16)


def scatter(blocks, s):
    ahead, back, across = ring(s), ring(-s), pair()
    move = lambda value, way: lax.ppermute(value, "fsdp", way)
    behind, before = -s % X, s % X
    with jax.named_scope("sum_far_other"):
        far_other = move(blocks[X + 2], back)
    with jax.named_scope("sum_near_other"):
        near_other = move(blocks[X + before], ahead)
    with jax.named_scope("sum_far"):
        far = move(after(blocks[2], far_other), back)
    with jax.named_scope("sum_near"):
        near = move(after(blocks[before], near_other), ahead)
    with jax.named_scope("sum_cross_side"):
        cross_side = move(add(blocks[X + behind], far_other), across)
    with jax.named_scope("sum_cross"):
        cross = move(add(blocks[X], near_other), across)
    with jax.named_scope("sum_side"):
        side = move(add(blocks[behind], far, cross_side), back)
    return [blocks[0], near, cross, side]


def per_device(
    inputs,
    targets,
    token_ids,
    path_weights,
    stale_deltas,
    module_params,
    momentum,
    module_of_path,
    sharing_counts,
):
    weights, delta = path_weights[0], stale_deltas[0]
    features = weights.shape[1]
    modules = sharing_counts.shape[0]
    place = jnp.stack([lax.axis_index("path"), lax.axis_index("fsdp")]).astype(jnp.int32)
    width = features // 2

    pieces = [None, None]
    pieces[0], begun, other_left, other_far = gather_first(weights[:, :width])
    normed = norm(place, inputs[0])

    dealt = deal(place, delta)
    dealt = [dealt[0]] + [lax.ppermute(dealt[k], "path", along_y(k)) for k in range(1, Y)]
    late = after(weights, *begun, *dealt[1:])[:, width:]
    pieces[1], late_begun = gather_second(late, other_left, other_far)
    mine, theirs = place_sums(place, module_of_path, dealt, modules, [normed, *begun])
    sums = add(mine, lax.ppermute(theirs, "path", cores()))
    along_z = [[(z * Y + y) * CORES + c for z in range(Z_HI)] for y in range(Y) for c in range(CORES)]
    total = lax.psum_scatter(sums, "path", scatter_dimension=0, axis_index_groups=along_z, tiled=True)[0]

    mask = (token_ids[0] != 0).astype(jnp.float32)[:, None]
    blocks = grads(normed, targets[0], mask, weights, pieces[0], 0, width, EXTRA, late_begun)
    new_params, new_momentum, step = outer(
        sharing_counts,
        [total],
        jnp.swapaxes(module_params, 1, 2),
        jnp.swapaxes(momentum, 1, 2),
        [blocks[0], *pieces[1]],
    )
    steps = lax.all_gather(step, "path", axis=0)

    terms = scatter(blocks, 1)
    blocks = grads(normed, targets[0], mask, weights, pieces[1], 1, width, 0)
    late_terms = scatter(blocks, -1)
    out = final(place, module_of_path, weights, steps, terms, None, 0, width)
    out = final(place, module_of_path, weights, steps, late_terms, out, 1, width)
    return (out[None], jnp.swapaxes(new_params, 1, 2), jnp.swapaxes(new_momentum, 1, 2))


def solution(mesh):
    return jax.shard_map(
        per_device,
        mesh=mesh,
        in_specs=(
            P("path", "fsdp", None),
            P("path", "fsdp", None),
            P("path", "fsdp"),
            P("path", "fsdp", None),
            P("path", "fsdp", None),
            P(None, "fsdp", "path"),
            P(None, "fsdp", "path"),
            P(),
            P(),
        ),
        out_specs=(P("path", "fsdp", None), P(None, "fsdp", "path"), P(None, "fsdp", "path")),
        check_vma=False,
    )
```

```python
import functools
import math

import jax
import jax.numpy as jnp
from jax import lax
from jax.experimental import pallas as pl
from jax.experimental.pallas import tpu as pltpu
from jax.sharding import PartitionSpec as P

Z_HI, Y, CORES, Z_LO, X = 4, 4, 2, 2, 4
HALF = 64
TILE = 512
BASE = 32.0
EXTRA = 16
VMEM_LIMIT = 60 * 1024 * 1024
SMALL_LIMIT = 16 * 1024 * 1024


def ring(step):
    return [(z * X + x, z * X + (x + step) % X) for z in range(Z_LO) for x in range(X)]


def pair():
    return [(z * X + x, (1 - z) * X + x) for z in range(Z_LO) for x in range(X)]


def along_y(step):
    return [
        ((z * Y + y) * CORES + c, (z * Y + (y + step) % Y) * CORES + c)
        for z in range(Z_HI)
        for y in range(Y)
        for c in range(CORES)
    ]


def along_z(step):
    return [
        ((z * Y + y) * CORES + c, (((z + step) % Z_HI) * Y + y) * CORES + c)
        for z in range(Z_HI)
        for y in range(Y)
        for c in range(CORES)
    ]


def cores():
    return [(p, p ^ 1) for p in range(Z_HI * Y * CORES)]


def owner(place, k):
    own_z, own_x = place // X, place % X
    return ((own_z + k // X) % Z_LO) * X + (own_x + k % X) % X


def norm_kernel(place_ref, x_ref, n_ref):
    values = x_ref[...].astype(jnp.float32)
    scale = lax.rsqrt(jnp.mean(values * values, axis=-1, keepdims=True) + 1e-06)
    width = x_ref.shape[1] // (Z_LO * X)
    for k in range(Z_LO * X):
        start = pl.multiple_of(owner(place_ref[1], k) * width, width)
        block = x_ref[:, pl.ds(start, width)].astype(jnp.float32) * scale
        n_ref[:, k * width : (k + 1) * width] = block.astype(jnp.bfloat16)


def norm(place, x):
    rows, width = x.shape
    step = 128
    block = pl.BlockSpec((step, width), lambda i, s: (i, 0))
    return pl.pallas_call(
        norm_kernel,
        grid_spec=pltpu.PrefetchScalarGridSpec(
            num_scalar_prefetch=1, grid=(rows // step,), in_specs=[block], out_specs=block
        ),
        out_shape=jax.ShapeDtypeStruct((rows, width), jnp.bfloat16),
        compiler_params=pltpu.CompilerParams(vmem_limit_bytes=SMALL_LIMIT),
        cost_estimate=pl.CostEstimate(flops=3 * rows * width, bytes_accessed=4 * rows * width, transcendentals=rows),
        name="norm",
    )(place, x)


def grad_kernel(n_ref, target_ref, mask_ref, *rest):
    pieces, outs, w_ref = rest[:8], rest[-9:-1], rest[-1]
    depth = pieces[0].shape[0]
    for k, piece in enumerate(pieces):
        w_ref[k * depth : (k + 1) * depth, :] = piece[...]
    projected = jnp.dot(n_ref[...], w_ref[...], preferred_element_type=jnp.float32)
    projected = projected * (1.0 / math.sqrt(n_ref.shape[1]))
    rows = ((projected - target_ref[...].astype(jnp.float32)) * mask_ref[...]).astype(jnp.bfloat16)
    for k, out in enumerate(outs):
        out[:depth, :] = lax.dot_general(
            n_ref[:, k * depth : (k + 1) * depth],
            rows,
            (((0,), (0,)), ((), ())),
            preferred_element_type=jnp.float32,
        ).astype(jnp.bfloat16)
    more = outs[0].shape[0] - depth
    if more:
        count = jnp.sum(mask_ref[...])
        high = jnp.floor(count * (1.0 / BASE))
        low = count - BASE * high
        upper = lax.broadcasted_iota(jnp.int32, (more, TILE), 0) < more // 2
        for out in outs:
            out[depth:, :] = jnp.where(upper, high, low).astype(jnp.bfloat16)


def grads(normed, targets, mask, weights, pieces, chunk, width, more, deps=()):
    rows, features = normed.shape
    depth = weights.shape[0]
    steps = width // TILE
    base = chunk * steps
    piece = pl.BlockSpec((depth, TILE), lambda j: (0, j))
    out = pl.BlockSpec((depth + more, TILE), lambda j: (0, j))
    return pl.pallas_call(
        grad_kernel,
        grid=(steps,),
        in_specs=[
            pl.BlockSpec((rows, features), lambda j: (0, 0), pipeline_mode=pl.Buffered(1)),
            pl.BlockSpec((rows, TILE), lambda j: (0, base + j)),
            pl.BlockSpec((rows, 1), lambda j: (0, 0), pipeline_mode=pl.Buffered(1)),
            pl.BlockSpec((depth, TILE), lambda j: (0, base + j)),
        ]
        + [piece] * 7
        + [pl.BlockSpec(memory_space=pl.ANY)] * len(deps),
        out_specs=[out] * 8,
        out_shape=[jax.ShapeDtypeStruct((depth + more, width), jnp.bfloat16)] * 8,
        scratch_shapes=[pltpu.VMEM((features, TILE), jnp.bfloat16)],
        compiler_params=pltpu.CompilerParams(vmem_limit_bytes=VMEM_LIMIT),
        cost_estimate=pl.CostEstimate(
            flops=4 * rows * features * width,
            bytes_accessed=2 * rows * features + 4 * features * width + 2 * rows * width,
            transcendentals=0,
        ),
        name="grads",
    )(normed, targets, mask, weights, *pieces, *deps)


def deal_kernel(place_ref, *refs):
    for source, out in zip(refs[:Y], refs[Y:]):
        out[0] = source[...]


def deal(place, delta):
    rows = delta.shape[0]
    lanes = CORES * HALF

    def at(step):
        return lambda z, s: (0, z * Y + (s[0] // CORES + step) % Y)

    return pl.pallas_call(
        deal_kernel,
        grid_spec=pltpu.PrefetchScalarGridSpec(
            num_scalar_prefetch=1,
            grid=(Z_HI,),
            in_specs=[pl.BlockSpec((rows, lanes), at(step)) for step in range(Y)],
            out_specs=[pl.BlockSpec((1, rows, lanes), lambda z, s: (z, 0, 0))] * Y,
        ),
        out_shape=[jax.ShapeDtypeStruct((Z_HI, rows, lanes), jnp.bfloat16)] * Y,
        compiler_params=pltpu.CompilerParams(vmem_limit_bytes=SMALL_LIMIT),
        cost_estimate=pl.CostEstimate(flops=0, bytes_accessed=4 * delta.size, transcendentals=0),
        name="deal",
    )(place, *[delta] * Y)


def halves(value):
    rows = value.shape[0] // 2
    top, bottom = value[:rows], value[rows:]
    left = lax.broadcasted_iota(jnp.int32, top.shape, 1) < HALF
    first = jnp.where(left, top, pltpu.roll(bottom, HALF, 1))
    second = jnp.where(left, pltpu.roll(top, HALF, 1), bottom)
    return first, second


def place_kernel(place_ref, module_ref, *refs):
    sources, mine, theirs = refs[:Y], refs[-2], refs[-1]
    path = place_ref[0]
    core, own_y, own_z = path % CORES, (path // CORES) % Y, path // (CORES * Y)
    values = [source[0].astype(jnp.float32) for source in sources]
    labels = [module_ref[(own_z * Y + (own_y + Y - step) % Y) * CORES + core] for step in range(Y)]
    for m in range(mine.shape[1]):
        total = jnp.zeros_like(values[0])
        for value, label in zip(values, labels):
            total = total + jnp.where(label == m, 1.0, 0.0) * value
        first, second = halves(total)
        mine[0, m] = jnp.where(core == 0, first, second).astype(jnp.bfloat16)
        theirs[0, m] = jnp.where(core == 0, second, first).astype(jnp.bfloat16)


def place_sums(place, module_of_path, sources, modules, deps):
    zs, rows, lanes = sources[0].shape

    return pl.pallas_call(
        place_kernel,
        grid_spec=pltpu.PrefetchScalarGridSpec(
            num_scalar_prefetch=2,
            grid=(zs,),
            in_specs=[pl.BlockSpec((1, rows, lanes), lambda z, s, t: (z, 0, 0))] * Y
            + [pl.BlockSpec(memory_space=pl.ANY)] * len(deps),
            out_specs=[pl.BlockSpec((1, modules, rows // 2, lanes), lambda z, s, t: (z, 0, 0, 0))] * 2,
        ),
        out_shape=[jax.ShapeDtypeStruct((zs, modules, rows // 2, lanes), jnp.bfloat16)] * 2,
        compiler_params=pltpu.CompilerParams(vmem_limit_bytes=SMALL_LIMIT),
        cost_estimate=pl.CostEstimate(
            flops=8 * modules * zs * rows * lanes, bytes_accessed=16 * zs * rows * lanes, transcendentals=0
        ),
        name="place_sums",
    )(place, module_of_path, *sources, *deps)


def outer_kernel(sources, count_ref, *refs):
    parts = refs[:sources]
    params_ref, momentum_ref = refs[sources : sources + 2]
    params_out, momentum_out, step_out = refs[-3:]
    count = count_ref[pl.program_id(0)].astype(jnp.float32)
    total = parts[0][0].astype(jnp.float32)
    for part in parts[1:]:
        total = total + part[0].astype(jnp.float32)
    turned = total.T
    total = jnp.concatenate([turned[:HALF], turned[HALF:]], axis=1)
    outer_grad = total / count
    new_momentum = 0.9 * momentum_ref[0] + outer_grad
    step = 0.7 * (outer_grad + 0.9 * new_momentum)
    momentum_out[0] = new_momentum
    params_out[0] = params_ref[0] - step
    rows = step.shape[1] // 2
    step_out[0] = jnp.concatenate([step[:, :rows], step[:, rows:]], axis=0).T.astype(jnp.bfloat16)


def outer(sharing_counts, parts, params, momentum):
    modules, columns, rows = params.shape
    state = pl.BlockSpec((1, columns, rows), lambda m, s: (m, 0, 0))
    packed = pl.BlockSpec((1,) + parts[0].shape[1:], lambda m, s: (m, 0, 0))
    return pl.pallas_call(
        functools.partial(outer_kernel, len(parts)),
        grid_spec=pltpu.PrefetchScalarGridSpec(
            num_scalar_prefetch=1,
            grid=(modules,),
            in_specs=[packed] * len(parts) + [state, state],
            out_specs=[state, state, packed],
        ),
        out_shape=[
            jax.ShapeDtypeStruct(params.shape, jnp.float32),
            jax.ShapeDtypeStruct(params.shape, jnp.float32),
            jax.ShapeDtypeStruct(parts[0].shape, jnp.bfloat16),
        ],
        compiler_params=pltpu.CompilerParams(vmem_limit_bytes=SMALL_LIMIT),
        cost_estimate=pl.CostEstimate(flops=8 * params.size, bytes_accessed=32 * params.size, transcendentals=0),
        name="outer",
    )(sharing_counts, *parts, params, momentum)


def final_kernel(terms, first_chunk, place_ref, module_ref, weight_ref, step_ref, *refs):
    depth = weight_ref.shape[0]
    grad = refs[0][...].astype(jnp.float32)
    for term in refs[1:terms]:
        grad = grad + term[...].astype(jnp.float32)
    if first_chunk:
        out, rate_out = refs[-2:]
        half = (grad.shape[0] - depth) // 2
        count = BASE * grad[depth : depth + half, :128] + grad[depth + half :, :128]
        rate_out[...] = 0.25 / jnp.sqrt(count)
        rate, grad = rate_out[0:1, 0:1], grad[:depth]
    else:
        rate, out = refs[terms][0:1, 0:1], refs[-1]
    inner = weight_ref[...].astype(jnp.float32) - rate * grad
    rows = step_ref.shape[3]
    left = lax.broadcasted_iota(jnp.int32, (rows, CORES * HALF), 1) < HALF
    for k in range(step_ref.shape[0] // CORES):
        first = step_ref[CORES * k, 0, 0].astype(jnp.float32)
        second = step_ref[CORES * k + 1, 0, 0].astype(jnp.float32)
        top = jnp.where(left, first, pltpu.roll(second, HALF, 1))
        bottom = jnp.where(left, pltpu.roll(first, HALF, 1), second)
        span = slice(k * CORES * HALF, (k + 1) * CORES * HALF)
        out[:rows, span] = (inner[:rows, span] - top).astype(jnp.bfloat16)
        out[rows:, span] = (inner[rows:, span] - bottom).astype(jnp.bfloat16)


def final(place, module_of_path, weights, steps, terms, earlier, chunk, width):
    depth, features = weights.shape
    grid = width // TILE
    base = chunk * grid
    rows, lanes = steps.shape[3:]

    def away(j, s, t):
        return (0, (s[0] // (CORES * Y) + Z_HI - (base + j)) % Z_HI, t[s[0]], 0, 0)

    first = earlier is None
    rate = pl.BlockSpec((8, 128), lambda j, s, t: (0, 0))
    extra = [] if first else [rate, pl.BlockSpec(memory_space=pl.ANY)]
    out = pl.BlockSpec((depth, TILE), lambda j, s, t: (0, base + j))
    result = jax.ShapeDtypeStruct((depth, features), jnp.bfloat16)
    return pl.pallas_call(
        functools.partial(final_kernel, len(terms), first),
        grid_spec=pltpu.PrefetchScalarGridSpec(
            num_scalar_prefetch=2,
            grid=(grid,),
            in_specs=[
                pl.BlockSpec((depth, TILE), lambda j, s, t: (0, base + j)),
                pl.BlockSpec((CORES * Y, 1, 1, rows, lanes), away),
            ]
            + [pl.BlockSpec((terms[0].shape[0], TILE), lambda j, s, t: (0, j))] * len(terms)
            + extra,
            out_specs=[out, rate] if first else out,
        ),
        out_shape=[result, jax.ShapeDtypeStruct((8, 128), jnp.float32)] if first else result,
        input_output_aliases={} if first else {5 + len(terms): 0},
        compiler_params=pltpu.CompilerParams(vmem_limit_bytes=SMALL_LIMIT),
        cost_estimate=pl.CostEstimate(flops=8 * depth * width, bytes_accessed=14 * depth * width, transcendentals=0),
        name="final",
    )(place, module_of_path, weights, steps, *terms, *([] if first else [earlier[1], earlier[0]]))


def after(value, *deps):
    return lax.optimization_barrier((value,) + deps)[0]


def shift(value, way):
    return lax.ppermute(value, "fsdp", way)


def by_offset(s, left, right, far, other, other_left, other_right, other_far):
    pieces = [None] * 8
    pieces[-s % X], pieces[s % X], pieces[2] = left, right, far
    pieces[X], pieces[X + -s % X], pieces[X + s % X], pieces[X + 2] = other, other_left, other_right, other_far
    return pieces[1:]


def gather_first(own):
    up, down, across = ring(1), ring(-1), pair()
    with jax.named_scope("shards"):
        left, right, other = shift(own, up), shift(own, down), shift(own, across)
    begun = (left, right, other)
    with jax.named_scope("shards_on"):
        far = shift(after(left, right, other), up)
        other_right = shift(after(other, left, right), down)
        other_left = shift(after(left, right, other), across)
    with jax.named_scope("shards_last"):
        other_far = shift(after(other_left, far), up)
    return by_offset(1, left, right, far, other, other_left, other_right, other_far), begun, other_left, other_far


def gather_second(own, other_left_a, other_far_a, sums):
    up, down, across = ring(1), ring(-1), pair()
    with jax.named_scope("late_shards"):
        left = shift(own, down)
        other = shift(after(own, other_left_a, sums), across)
        right = shift(after(own, other_far_a), up)
    with jax.named_scope("late_shards_on"):
        far, other_left, other_right = shift(left, down), shift(left, across), shift(other, up)
    with jax.named_scope("late_shards_last"):
        other_far = shift(other_left, down)
    return by_offset(-1, left, right, far, other, other_left, other_right, other_far), (left, other)


def add(*values):
    total = values[0].astype(jnp.float32)
    for value in values[1:]:
        total = total + value.astype(jnp.float32)
    return total.astype(jnp.bfloat16)


def scatter(blocks, s):
    ahead, back, across = ring(s), ring(-s), pair()
    move = lambda value, way: lax.ppermute(value, "fsdp", way)
    behind, before = -s % X, s % X
    with jax.named_scope("sum_far_other"):
        far_other = move(blocks[X + 2], back)
    with jax.named_scope("sum_near_other"):
        near_other = move(blocks[X + before], ahead)
    with jax.named_scope("sum_far"):
        far = move(after(blocks[2], far_other), back)
    with jax.named_scope("sum_near"):
        near = move(after(blocks[before], near_other), ahead)
    with jax.named_scope("sum_cross_side"):
        cross_side = move(add(blocks[X + behind], far_other), across)
    with jax.named_scope("sum_cross"):
        cross = move(add(blocks[X], near_other), across)
    with jax.named_scope("sum_side"):
        side = move(add(blocks[behind], far, cross_side), back)
    return [blocks[0], near, cross, side], (far_other, near_other)


def per_device(
    inputs,
    targets,
    token_ids,
    path_weights,
    stale_deltas,
    module_params,
    momentum,
    module_of_path,
    sharing_counts,
):
    weights, delta = path_weights[0], stale_deltas[0]
    features = weights.shape[1]
    modules = sharing_counts.shape[0]
    place = jnp.stack([lax.axis_index("path"), lax.axis_index("fsdp")]).astype(jnp.int32)
    width = features // 2

    pieces = [None, None]
    pieces[0], begun, other_left, other_far = gather_first(weights[:, :width])
    normed = norm(place, inputs[0])

    dealt = deal(place, delta)
    dealt = [dealt[0]] + [lax.ppermute(dealt[k], "path", along_y(k)) for k in range(1, Y)]
    late = after(weights, *begun, *dealt[1:])[:, width:]
    mine, theirs = place_sums(place, module_of_path, dealt, modules, [normed, *begun])
    sums = add(mine, lax.ppermute(theirs, "path", cores()))
    pieces[1], late_begun = gather_second(late, other_left, other_far, sums)
    columns = [[(z * Y + y) * CORES + c for z in range(Z_HI)] for y in range(Y) for c in range(CORES)]
    total = lax.psum_scatter(sums, "path", scatter_dimension=0, axis_index_groups=columns, tiled=True)[0]

    mask = (token_ids[0] != 0).astype(jnp.float32)[:, None]
    blocks = grads(normed, targets[0], mask, weights, pieces[0], 0, width, EXTRA, late_begun)
    new_params, new_momentum, step = outer(
        after(sharing_counts, blocks[0], *pieces[1]),
        [total],
        jnp.swapaxes(module_params, 1, 2),
        jnp.swapaxes(momentum, 1, 2),
    )
    with jax.named_scope("steps_along_z"):
        steps = [step] + [lax.ppermute(step, "path", along_z(k)) for k in range(1, Z_HI)]
    terms, begun = scatter(blocks, 1)
    blocks = grads(normed, targets[0], mask, weights, pieces[1], 1, width, 0)
    planes = [[(z * Y + y) * CORES + c for y in range(Y) for c in range(CORES)] for z in range(Z_HI)]
    steps = after(jnp.stack(steps), blocks[0], *begun)
    steps = lax.all_gather(steps, "path", axis=0, axis_index_groups=planes)
    late_terms, _ = scatter(blocks, -1)
    out = final(place, module_of_path, weights, steps, terms, None, 0, width)
    out = final(place, module_of_path, weights, steps, late_terms, out, 1, width)
    return (out[None], jnp.swapaxes(new_params, 1, 2), jnp.swapaxes(new_momentum, 1, 2))


def solution(mesh):
    return jax.shard_map(
        per_device,
        mesh=mesh,
        in_specs=(
            P("path", "fsdp", None),
            P("path", "fsdp", None),
            P("path", "fsdp"),
            P("path", "fsdp", None),
            P("path", "fsdp", None),
            P(None, "fsdp", "path"),
            P(None, "fsdp", "path"),
            P(),
            P(),
        ),
        out_specs=(P("path", "fsdp", None), P(None, "fsdp", "path"), P(None, "fsdp", "path")),
        check_vma=False,
    )
```

```python
import functools
import math

import jax
import jax.numpy as jnp
from jax import lax
from jax.experimental import pallas as pl
from jax.experimental.pallas import tpu as pltpu
from jax.sharding import PartitionSpec as P

Z_HI, Y, CORES, Z_LO, X = 4, 4, 2, 2, 4
HALF = 64
TILE = 512
BASE = 32.0
EXTRA = 16
VMEM_LIMIT = 60 * 1024 * 1024
SMALL_LIMIT = 16 * 1024 * 1024


def ring(step):
    return [(z * X + x, z * X + (x + step) % X) for z in range(Z_LO) for x in range(X)]


def pair():
    return [(z * X + x, (1 - z) * X + x) for z in range(Z_LO) for x in range(X)]


def along_y(step):
    return [
        ((z * Y + y) * CORES + c, (z * Y + (y + step) % Y) * CORES + c)
        for z in range(Z_HI)
        for y in range(Y)
        for c in range(CORES)
    ]


def along_z(step):
    return [
        ((z * Y + y) * CORES + c, (((z + step) % Z_HI) * Y + y) * CORES + c)
        for z in range(Z_HI)
        for y in range(Y)
        for c in range(CORES)
    ]


def cores():
    return [(p, p ^ 1) for p in range(Z_HI * Y * CORES)]


def owner(place, k):
    own_z, own_x = place // X, place % X
    return ((own_z + k // X) % Z_LO) * X + (own_x + k % X) % X


def norm_kernel(place_ref, x_ref, n_ref):
    values = x_ref[...].astype(jnp.float32)
    scale = lax.rsqrt(jnp.mean(values * values, axis=-1, keepdims=True) + 1e-06)
    width = x_ref.shape[1] // (Z_LO * X)
    for k in range(Z_LO * X):
        start = pl.multiple_of(owner(place_ref[1], k) * width, width)
        block = x_ref[:, pl.ds(start, width)].astype(jnp.float32) * scale
        n_ref[:, k * width : (k + 1) * width] = block.astype(jnp.bfloat16)


def norm(place, x):
    rows, width = x.shape
    step = 128
    block = pl.BlockSpec((step, width), lambda i, s: (i, 0))
    return pl.pallas_call(
        norm_kernel,
        grid_spec=pltpu.PrefetchScalarGridSpec(
            num_scalar_prefetch=1, grid=(rows // step,), in_specs=[block], out_specs=block
        ),
        out_shape=jax.ShapeDtypeStruct((rows, width), jnp.bfloat16),
        compiler_params=pltpu.CompilerParams(vmem_limit_bytes=SMALL_LIMIT),
        cost_estimate=pl.CostEstimate(flops=3 * rows * width, bytes_accessed=4 * rows * width, transcendentals=rows),
        name="norm",
    )(place, x)


def grad_kernel(n_ref, target_ref, mask_ref, *rest):
    pieces, outs, w_ref = rest[:8], rest[-9:-1], rest[-1]
    depth = pieces[0].shape[0]
    for k, piece in enumerate(pieces):
        w_ref[k * depth : (k + 1) * depth, :] = piece[...]
    projected = jnp.dot(n_ref[...], w_ref[...], preferred_element_type=jnp.float32)
    projected = projected * (1.0 / math.sqrt(n_ref.shape[1]))
    rows = ((projected - target_ref[...].astype(jnp.float32)) * mask_ref[...]).astype(jnp.bfloat16)
    for k, out in enumerate(outs):
        out[:depth, :] = lax.dot_general(
            n_ref[:, k * depth : (k + 1) * depth],
            rows,
            (((0,), (0,)), ((), ())),
            preferred_element_type=jnp.float32,
        ).astype(jnp.bfloat16)
    more = outs[0].shape[0] - depth
    if more:
        count = jnp.sum(mask_ref[...])
        high = jnp.floor(count * (1.0 / BASE))
        low = count - BASE * high
        upper = lax.broadcasted_iota(jnp.int32, (more, TILE), 0) < more // 2
        for out in outs:
            out[depth:, :] = jnp.where(upper, high, low).astype(jnp.bfloat16)


def grads(normed, targets, mask, weights, pieces, chunk, width, more, deps=()):
    rows, features = normed.shape
    depth = weights.shape[0]
    steps = width // TILE
    base = chunk * steps
    piece = pl.BlockSpec((depth, TILE), lambda j: (0, j))
    out = pl.BlockSpec((depth + more, TILE), lambda j: (0, j))
    return pl.pallas_call(
        grad_kernel,
        grid=(steps,),
        in_specs=[
            pl.BlockSpec((rows, features), lambda j: (0, 0), pipeline_mode=pl.Buffered(1)),
            pl.BlockSpec((rows, TILE), lambda j: (0, base + j)),
            pl.BlockSpec((rows, 1), lambda j: (0, 0), pipeline_mode=pl.Buffered(1)),
            pl.BlockSpec((depth, TILE), lambda j: (0, base + j)),
        ]
        + [piece] * 7
        + [pl.BlockSpec(memory_space=pl.ANY)] * len(deps),
        out_specs=[out] * 8,
        out_shape=[jax.ShapeDtypeStruct((depth + more, width), jnp.bfloat16)] * 8,
        scratch_shapes=[pltpu.VMEM((features, TILE), jnp.bfloat16)],
        compiler_params=pltpu.CompilerParams(vmem_limit_bytes=VMEM_LIMIT),
        cost_estimate=pl.CostEstimate(
            flops=4 * rows * features * width,
            bytes_accessed=2 * rows * features + 4 * features * width + 2 * rows * width,
            transcendentals=0,
        ),
        name="grads",
    )(normed, targets, mask, weights, *pieces, *deps)


def deal_kernel(place_ref, *refs):
    for source, out in zip(refs[:Y], refs[Y:]):
        out[0] = source[...]


def deal(place, delta):
    rows = delta.shape[0]
    lanes = CORES * HALF

    def at(step):
        return lambda z, s: (0, z * Y + (s[0] // CORES + step) % Y)

    return pl.pallas_call(
        deal_kernel,
        grid_spec=pltpu.PrefetchScalarGridSpec(
            num_scalar_prefetch=1,
            grid=(Z_HI,),
            in_specs=[pl.BlockSpec((rows, lanes), at(step)) for step in range(Y)],
            out_specs=[pl.BlockSpec((1, rows, lanes), lambda z, s: (z, 0, 0))] * Y,
        ),
        out_shape=[jax.ShapeDtypeStruct((Z_HI, rows, lanes), jnp.bfloat16)] * Y,
        compiler_params=pltpu.CompilerParams(vmem_limit_bytes=SMALL_LIMIT),
        cost_estimate=pl.CostEstimate(flops=0, bytes_accessed=4 * delta.size, transcendentals=0),
        name="deal",
    )(place, *[delta] * Y)


def halves(value):
    rows = value.shape[0] // 2
    top, bottom = value[:rows], value[rows:]
    left = lax.broadcasted_iota(jnp.int32, top.shape, 1) < HALF
    first = jnp.where(left, top, pltpu.roll(bottom, HALF, 1))
    second = jnp.where(left, pltpu.roll(top, HALF, 1), bottom)
    return first, second


def place_kernel(place_ref, module_ref, *refs):
    sources, mine, theirs = refs[:Y], refs[-2], refs[-1]
    path = place_ref[0]
    core, own_y, own_z = path % CORES, (path // CORES) % Y, path // (CORES * Y)
    values = [source[0].astype(jnp.float32) for source in sources]
    labels = [module_ref[(own_z * Y + (own_y + Y - step) % Y) * CORES + core] for step in range(Y)]
    for m in range(mine.shape[1]):
        total = jnp.zeros_like(values[0])
        for value, label in zip(values, labels):
            total = total + jnp.where(label == m, 1.0, 0.0) * value
        first, second = halves(total)
        mine[0, m] = jnp.where(core == 0, first, second).astype(jnp.bfloat16)
        theirs[0, m] = jnp.where(core == 0, second, first).astype(jnp.bfloat16)


def place_sums(place, module_of_path, sources, modules, deps):
    zs, rows, lanes = sources[0].shape

    return pl.pallas_call(
        place_kernel,
        grid_spec=pltpu.PrefetchScalarGridSpec(
            num_scalar_prefetch=2,
            grid=(zs,),
            in_specs=[pl.BlockSpec((1, rows, lanes), lambda z, s, t: (z, 0, 0))] * Y
            + [pl.BlockSpec(memory_space=pl.ANY)] * len(deps),
            out_specs=[pl.BlockSpec((1, modules, rows // 2, lanes), lambda z, s, t: (z, 0, 0, 0))] * 2,
        ),
        out_shape=[jax.ShapeDtypeStruct((zs, modules, rows // 2, lanes), jnp.bfloat16)] * 2,
        compiler_params=pltpu.CompilerParams(vmem_limit_bytes=SMALL_LIMIT),
        cost_estimate=pl.CostEstimate(
            flops=8 * modules * zs * rows * lanes, bytes_accessed=16 * zs * rows * lanes, transcendentals=0
        ),
        name="place_sums",
    )(place, module_of_path, *sources, *deps)


def outer_kernel(sources, count_ref, *refs):
    parts = refs[:sources]
    params_ref, momentum_ref = refs[sources : sources + 2]
    params_out, momentum_out, step_out = refs[-3:]
    count = count_ref[pl.program_id(0)].astype(jnp.float32)
    total = parts[0][0].astype(jnp.float32)
    for part in parts[1:]:
        total = total + part[0].astype(jnp.float32)
    turned = total.T
    total = jnp.concatenate([turned[:HALF], turned[HALF:]], axis=1)
    outer_grad = total / count
    new_momentum = 0.9 * momentum_ref[0] + outer_grad
    step = 0.7 * (outer_grad + 0.9 * new_momentum)
    momentum_out[0] = new_momentum
    params_out[0] = params_ref[0] - step
    rows = step.shape[1] // 2
    step_out[0] = jnp.concatenate([step[:, :rows], step[:, rows:]], axis=0).T.astype(jnp.bfloat16)


def outer(sharing_counts, parts, params, momentum):
    modules, columns, rows = params.shape
    state = pl.BlockSpec((1, columns, rows), lambda m, s: (m, 0, 0))
    packed = pl.BlockSpec((1,) + parts[0].shape[1:], lambda m, s: (m, 0, 0))
    return pl.pallas_call(
        functools.partial(outer_kernel, len(parts)),
        grid_spec=pltpu.PrefetchScalarGridSpec(
            num_scalar_prefetch=1,
            grid=(modules,),
            in_specs=[packed] * len(parts) + [state, state],
            out_specs=[state, state, packed],
        ),
        out_shape=[
            jax.ShapeDtypeStruct(params.shape, jnp.float32),
            jax.ShapeDtypeStruct(params.shape, jnp.float32),
            jax.ShapeDtypeStruct(parts[0].shape, jnp.bfloat16),
        ],
        compiler_params=pltpu.CompilerParams(vmem_limit_bytes=SMALL_LIMIT),
        cost_estimate=pl.CostEstimate(flops=8 * params.size, bytes_accessed=32 * params.size, transcendentals=0),
        name="outer",
    )(sharing_counts, *parts, params, momentum)


def final_kernel(terms, first_chunk, place_ref, module_ref, weight_ref, step_ref, *refs):
    depth = weight_ref.shape[0]
    grad = refs[0][...].astype(jnp.float32)
    for term in refs[1:terms]:
        grad = grad + term[...].astype(jnp.float32)
    if first_chunk:
        out, rate_out = refs[-2:]
        half = (grad.shape[0] - depth) // 2
        count = BASE * grad[depth : depth + half, :128] + grad[depth + half :, :128]
        rate_out[...] = 0.25 / jnp.sqrt(count)
        rate, grad = rate_out[0:1, 0:1], grad[:depth]
    else:
        rate, out = refs[terms][0:1, 0:1], refs[-1]
    inner = weight_ref[...].astype(jnp.float32) - rate * grad
    rows = step_ref.shape[3]
    left = lax.broadcasted_iota(jnp.int32, (rows, CORES * HALF), 1) < HALF
    for k in range(step_ref.shape[0] // CORES):
        first = step_ref[CORES * k, 0, 0].astype(jnp.float32)
        second = step_ref[CORES * k + 1, 0, 0].astype(jnp.float32)
        top = jnp.where(left, first, pltpu.roll(second, HALF, 1))
        bottom = jnp.where(left, pltpu.roll(first, HALF, 1), second)
        span = slice(k * CORES * HALF, (k + 1) * CORES * HALF)
        out[:rows, span] = (inner[:rows, span] - top).astype(jnp.bfloat16)
        out[rows:, span] = (inner[rows:, span] - bottom).astype(jnp.bfloat16)


def final(place, module_of_path, weights, steps, terms, earlier, chunk, width):
    depth, features = weights.shape
    grid = width // TILE
    base = chunk * grid
    rows, lanes = steps.shape[3:]

    def away(j, s, t):
        return (0, (s[0] // (CORES * Y) + Z_HI - (base + j)) % Z_HI, t[s[0]], 0, 0)

    first = earlier is None
    rate = pl.BlockSpec((8, 128), lambda j, s, t: (0, 0))
    extra = [] if first else [rate, pl.BlockSpec(memory_space=pl.ANY)]
    out = pl.BlockSpec((depth, TILE), lambda j, s, t: (0, base + j))
    result = jax.ShapeDtypeStruct((depth, features), jnp.bfloat16)
    return pl.pallas_call(
        functools.partial(final_kernel, len(terms), first),
        grid_spec=pltpu.PrefetchScalarGridSpec(
            num_scalar_prefetch=2,
            grid=(grid,),
            in_specs=[
                pl.BlockSpec((depth, TILE), lambda j, s, t: (0, base + j)),
                pl.BlockSpec((CORES * Y, 1, 1, rows, lanes), away),
            ]
            + [pl.BlockSpec((terms[0].shape[0], TILE), lambda j, s, t: (0, j))] * len(terms)
            + extra,
            out_specs=[out, rate] if first else out,
        ),
        out_shape=[result, jax.ShapeDtypeStruct((8, 128), jnp.float32)] if first else result,
        input_output_aliases={} if first else {5 + len(terms): 0},
        compiler_params=pltpu.CompilerParams(vmem_limit_bytes=SMALL_LIMIT),
        cost_estimate=pl.CostEstimate(flops=8 * depth * width, bytes_accessed=14 * depth * width, transcendentals=0),
        name="final",
    )(place, module_of_path, weights, steps, *terms, *([] if first else [earlier[1], earlier[0]]))


def after(value, *deps):
    return lax.optimization_barrier((value,) + deps)[0]


def shift(value, way):
    return lax.ppermute(value, "fsdp", way)


def by_offset(s, left, right, far, other, other_left, other_right, other_far):
    pieces = [None] * 8
    pieces[-s % X], pieces[s % X], pieces[2] = left, right, far
    pieces[X], pieces[X + -s % X], pieces[X + s % X], pieces[X + 2] = other, other_left, other_right, other_far
    return pieces[1:]


def gather_first(own):
    up, down, across = ring(1), ring(-1), pair()
    with jax.named_scope("shards"):
        left, right, other = shift(own, up), shift(own, down), shift(own, across)
    begun = (left, right, other)
    with jax.named_scope("shards_on"):
        far = shift(after(left, right, other), up)
        other_right = shift(after(other, left, right), down)
        other_left = shift(after(left, right, other), across)
    with jax.named_scope("shards_last"):
        other_far = shift(after(other_left, far, other_right), up)
    return by_offset(1, left, right, far, other, other_left, other_right, other_far), begun, other_left, other_far


def gather_second(own, other_left_a, other_far_a, sums):
    up, down, across = ring(1), ring(-1), pair()
    with jax.named_scope("late_shards"):
        left = shift(own, down)
        other = shift(after(own, other_left_a, sums), across)
        right = shift(after(own, other_far_a), up)
    with jax.named_scope("late_shards_on"):
        far, other_left, other_right = shift(left, down), shift(left, across), shift(other, up)
    with jax.named_scope("late_shards_last"):
        other_far = shift(other_left, down)
    return by_offset(-1, left, right, far, other, other_left, other_right, other_far), (left, other)


def add(*values):
    total = values[0].astype(jnp.float32)
    for value in values[1:]:
        total = total + value.astype(jnp.float32)
    return total.astype(jnp.bfloat16)


def scatter(blocks, s):
    ahead, back, across = ring(s), ring(-s), pair()
    move = lambda value, way: lax.ppermute(value, "fsdp", way)
    behind, before = -s % X, s % X
    with jax.named_scope("sum_far_other"):
        far_other = move(blocks[X + 2], back)
    with jax.named_scope("sum_near_other"):
        near_other = move(blocks[X + before], ahead)
    with jax.named_scope("sum_far"):
        far = move(after(blocks[2], far_other), back)
    with jax.named_scope("sum_near"):
        near = move(after(blocks[before], near_other), ahead)
    with jax.named_scope("sum_cross_side"):
        cross_side = move(add(blocks[X + behind], far_other), across)
    with jax.named_scope("sum_cross"):
        cross = move(add(blocks[X], near_other), across)
    with jax.named_scope("sum_side"):
        side = move(add(blocks[behind], far, cross_side), back)
    return [blocks[0], near, cross, side], (far_other, near_other)


def per_device(
    inputs,
    targets,
    token_ids,
    path_weights,
    stale_deltas,
    module_params,
    momentum,
    module_of_path,
    sharing_counts,
):
    weights, delta = path_weights[0], stale_deltas[0]
    features = weights.shape[1]
    modules = sharing_counts.shape[0]
    place = jnp.stack([lax.axis_index("path"), lax.axis_index("fsdp")]).astype(jnp.int32)
    width = features // 2

    pieces = [None, None]
    pieces[0], begun, other_left, other_far = gather_first(weights[:, :width])
    normed = norm(place, inputs[0])

    dealt = deal(place, delta)
    dealt = [dealt[0], dealt[1], after(dealt[2], normed), dealt[3]]
    dealt = [dealt[0]] + [lax.ppermute(dealt[k], "path", along_y(k)) for k in range(1, Y)]
    late = after(weights, *begun, *dealt[1:])[:, width:]
    mine, theirs = place_sums(place, module_of_path, dealt, modules, [normed, *begun])
    sums = add(mine, lax.ppermute(theirs, "path", cores()))
    pieces[1], late_begun = gather_second(late, other_left, other_far, sums)
    columns = [[(z * Y + y) * CORES + c for z in range(Z_HI)] for y in range(Y) for c in range(CORES)]
    total = lax.psum_scatter(sums, "path", scatter_dimension=0, axis_index_groups=columns, tiled=True)[0]

    mask = (token_ids[0] != 0).astype(jnp.float32)[:, None]
    blocks = grads(normed, targets[0], mask, weights, pieces[0], 0, width, EXTRA, late_begun)
    new_params, new_momentum, step = outer(
        after(sharing_counts, blocks[0], *pieces[1]),
        [total],
        jnp.swapaxes(module_params, 1, 2),
        jnp.swapaxes(momentum, 1, 2),
    )
    with jax.named_scope("steps_along_z"):
        steps = [step] + [lax.ppermute(step, "path", along_z(k)) for k in range(1, Z_HI)]
    terms, begun = scatter(blocks, 1)
    blocks = grads(normed, targets[0], mask, weights, pieces[1], 1, width, 0)
    planes = [[(z * Y + y) * CORES + c for y in range(Y) for c in range(CORES)] for z in range(Z_HI)]
    steps = after(jnp.stack(steps), blocks[0], *begun)
    steps = lax.all_gather(steps, "path", axis=0, axis_index_groups=planes)
    late_terms, _ = scatter(blocks, -1)
    out = final(place, module_of_path, weights, steps, terms, None, 0, width)
    out = final(place, module_of_path, weights, steps, late_terms, out, 1, width)
    return (out[None], jnp.swapaxes(new_params, 1, 2), jnp.swapaxes(new_momentum, 1, 2))


def solution(mesh):
    return jax.shard_map(
        per_device,
        mesh=mesh,
        in_specs=(
            P("path", "fsdp", None),
            P("path", "fsdp", None),
            P("path", "fsdp"),
            P("path", "fsdp", None),
            P("path", "fsdp", None),
            P(None, "fsdp", "path"),
            P(None, "fsdp", "path"),
            P(),
            P(),
        ),
        out_specs=(P("path", "fsdp", None), P(None, "fsdp", "path"), P(None, "fsdp", "path")),
        check_vma=False,
    )
```

```python
import functools
import math

import jax
import jax.numpy as jnp
from jax import lax
from jax.experimental import pallas as pl
from jax.experimental.pallas import tpu as pltpu
from jax.sharding import PartitionSpec as P

Z_HI, Y, CORES, Z_LO, X = 4, 4, 2, 2, 4
HALF = 64
TILE = 512
BASE = 32.0
EXTRA = 16
VMEM_LIMIT = 60 * 1024 * 1024
SMALL_LIMIT = 16 * 1024 * 1024


def ring(step):
    return [(z * X + x, z * X + (x + step) % X) for z in range(Z_LO) for x in range(X)]


def pair():
    return [(z * X + x, (1 - z) * X + x) for z in range(Z_LO) for x in range(X)]


def along_y(step):
    return [
        ((z * Y + y) * CORES + c, (z * Y + (y + step) % Y) * CORES + c)
        for z in range(Z_HI)
        for y in range(Y)
        for c in range(CORES)
    ]


def along_z(step):
    return [
        ((z * Y + y) * CORES + c, (((z + step) % Z_HI) * Y + y) * CORES + c)
        for z in range(Z_HI)
        for y in range(Y)
        for c in range(CORES)
    ]


def cores():
    return [(p, p ^ 1) for p in range(Z_HI * Y * CORES)]


def owner(place, k):
    own_z, own_x = place // X, place % X
    return ((own_z + k // X) % Z_LO) * X + (own_x + k % X) % X


def norm_kernel(place_ref, x_ref, n_ref):
    values = x_ref[...].astype(jnp.float32)
    scale = lax.rsqrt(jnp.mean(values * values, axis=-1, keepdims=True) + 1e-06)
    width = x_ref.shape[1] // (Z_LO * X)
    for k in range(Z_LO * X):
        start = pl.multiple_of(owner(place_ref[1], k) * width, width)
        block = x_ref[:, pl.ds(start, width)].astype(jnp.float32) * scale
        n_ref[:, k * width : (k + 1) * width] = block.astype(jnp.bfloat16)


def norm(place, x):
    rows, width = x.shape
    step = 128
    block = pl.BlockSpec((step, width), lambda i, s: (i, 0))
    return pl.pallas_call(
        norm_kernel,
        grid_spec=pltpu.PrefetchScalarGridSpec(
            num_scalar_prefetch=1, grid=(rows // step,), in_specs=[block], out_specs=block
        ),
        out_shape=jax.ShapeDtypeStruct((rows, width), jnp.bfloat16),
        compiler_params=pltpu.CompilerParams(vmem_limit_bytes=SMALL_LIMIT),
        cost_estimate=pl.CostEstimate(flops=3 * rows * width, bytes_accessed=4 * rows * width, transcendentals=rows),
        name="norm",
    )(place, x)


def grad_kernel(n_ref, target_ref, mask_ref, *rest):
    pieces, outs, w_ref = rest[:8], rest[-9:-1], rest[-1]
    depth = pieces[0].shape[0]
    for k, piece in enumerate(pieces):
        w_ref[k * depth : (k + 1) * depth, :] = piece[...]
    projected = jnp.dot(n_ref[...], w_ref[...], preferred_element_type=jnp.float32)
    projected = projected * (1.0 / math.sqrt(n_ref.shape[1]))
    rows = ((projected - target_ref[...].astype(jnp.float32)) * mask_ref[...]).astype(jnp.bfloat16)
    for k, out in enumerate(outs):
        out[:depth, :] = lax.dot_general(
            n_ref[:, k * depth : (k + 1) * depth],
            rows,
            (((0,), (0,)), ((), ())),
            preferred_element_type=jnp.float32,
        ).astype(jnp.bfloat16)
    more = outs[0].shape[0] - depth
    if more:
        count = jnp.sum(mask_ref[...])
        high = jnp.floor(count * (1.0 / BASE))
        low = count - BASE * high
        upper = lax.broadcasted_iota(jnp.int32, (more, TILE), 0) < more // 2
        for out in outs:
            out[depth:, :] = jnp.where(upper, high, low).astype(jnp.bfloat16)


def grads(normed, targets, mask, weights, pieces, chunk, width, more, deps=()):
    rows, features = normed.shape
    depth = weights.shape[0]
    steps = width // TILE
    base = chunk * steps
    piece = pl.BlockSpec((depth, TILE), lambda j: (0, j))
    out = pl.BlockSpec((depth + more, TILE), lambda j: (0, j))
    return pl.pallas_call(
        grad_kernel,
        grid=(steps,),
        in_specs=[
            pl.BlockSpec((rows, features), lambda j: (0, 0), pipeline_mode=pl.Buffered(1)),
            pl.BlockSpec((rows, TILE), lambda j: (0, base + j)),
            pl.BlockSpec((rows, 1), lambda j: (0, 0), pipeline_mode=pl.Buffered(1)),
            pl.BlockSpec((depth, TILE), lambda j: (0, base + j)),
        ]
        + [piece] * 7
        + [pl.BlockSpec(memory_space=pl.ANY)] * len(deps),
        out_specs=[out] * 8,
        out_shape=[jax.ShapeDtypeStruct((depth + more, width), jnp.bfloat16)] * 8,
        scratch_shapes=[pltpu.VMEM((features, TILE), jnp.bfloat16)],
        compiler_params=pltpu.CompilerParams(vmem_limit_bytes=VMEM_LIMIT),
        cost_estimate=pl.CostEstimate(
            flops=4 * rows * features * width,
            bytes_accessed=2 * rows * features + 4 * features * width + 2 * rows * width,
            transcendentals=0,
        ),
        name="grads",
    )(normed, targets, mask, weights, *pieces, *deps)


def deal_kernel(place_ref, *refs):
    for source, out in zip(refs[:Y], refs[Y:]):
        out[0] = source[...]


def deal(place, delta):
    rows = delta.shape[0]
    lanes = CORES * HALF

    def at(step):
        return lambda z, s: (0, z * Y + (s[0] // CORES + step) % Y)

    return pl.pallas_call(
        deal_kernel,
        grid_spec=pltpu.PrefetchScalarGridSpec(
            num_scalar_prefetch=1,
            grid=(Z_HI,),
            in_specs=[pl.BlockSpec((rows, lanes), at(step)) for step in range(Y)],
            out_specs=[pl.BlockSpec((1, rows, lanes), lambda z, s: (z, 0, 0))] * Y,
        ),
        out_shape=[jax.ShapeDtypeStruct((Z_HI, rows, lanes), jnp.bfloat16)] * Y,
        compiler_params=pltpu.CompilerParams(vmem_limit_bytes=SMALL_LIMIT),
        cost_estimate=pl.CostEstimate(flops=0, bytes_accessed=4 * delta.size, transcendentals=0),
        name="deal",
    )(place, *[delta] * Y)


def halves(value):
    rows = value.shape[0] // 2
    top, bottom = value[:rows], value[rows:]
    left = lax.broadcasted_iota(jnp.int32, top.shape, 1) < HALF
    first = jnp.where(left, top, pltpu.roll(bottom, HALF, 1))
    second = jnp.where(left, pltpu.roll(top, HALF, 1), bottom)
    return first, second


def place_kernel(place_ref, module_ref, *refs):
    sources, mine, theirs = refs[:Y], refs[-2], refs[-1]
    path = place_ref[0]
    core, own_y, own_z = path % CORES, (path // CORES) % Y, path // (CORES * Y)
    values = [source[0].astype(jnp.float32) for source in sources]
    labels = [module_ref[(own_z * Y + (own_y + Y - step) % Y) * CORES + core] for step in range(Y)]
    for m in range(mine.shape[1]):
        total = jnp.zeros_like(values[0])
        for value, label in zip(values, labels):
            total = total + jnp.where(label == m, 1.0, 0.0) * value
        first, second = halves(total)
        mine[0, m] = jnp.where(core == 0, first, second).astype(jnp.bfloat16)
        theirs[0, m] = jnp.where(core == 0, second, first).astype(jnp.bfloat16)


def place_sums(place, module_of_path, sources, modules, deps):
    zs, rows, lanes = sources[0].shape

    return pl.pallas_call(
        place_kernel,
        grid_spec=pltpu.PrefetchScalarGridSpec(
            num_scalar_prefetch=2,
            grid=(zs,),
            in_specs=[pl.BlockSpec((1, rows, lanes), lambda z, s, t: (z, 0, 0))] * Y
            + [pl.BlockSpec(memory_space=pl.ANY)] * len(deps),
            out_specs=[pl.BlockSpec((1, modules, rows // 2, lanes), lambda z, s, t: (z, 0, 0, 0))] * 2,
        ),
        out_shape=[jax.ShapeDtypeStruct((zs, modules, rows // 2, lanes), jnp.bfloat16)] * 2,
        compiler_params=pltpu.CompilerParams(vmem_limit_bytes=SMALL_LIMIT),
        cost_estimate=pl.CostEstimate(
            flops=8 * modules * zs * rows * lanes, bytes_accessed=16 * zs * rows * lanes, transcendentals=0
        ),
        name="place_sums",
    )(place, module_of_path, *sources, *deps)


def outer_kernel(sources, count_ref, *refs):
    parts = refs[:sources]
    params_ref, momentum_ref = refs[sources : sources + 2]
    params_out, momentum_out, step_out = refs[-3:]
    count = count_ref[pl.program_id(0)].astype(jnp.float32)
    total = parts[0][0].astype(jnp.float32)
    for part in parts[1:]:
        total = total + part[0].astype(jnp.float32)
    turned = total.T
    total = jnp.concatenate([turned[:HALF], turned[HALF:]], axis=1)
    outer_grad = total / count
    new_momentum = 0.9 * momentum_ref[0] + outer_grad
    step = 0.7 * (outer_grad + 0.9 * new_momentum)
    momentum_out[0] = new_momentum
    params_out[0] = params_ref[0] - step
    rows = step.shape[1] // 2
    step_out[0] = jnp.concatenate([step[:, :rows], step[:, rows:]], axis=0).T.astype(jnp.bfloat16)


def outer(sharing_counts, parts, params, momentum):
    modules, columns, rows = params.shape
    state = pl.BlockSpec((1, columns, rows), lambda m, s: (m, 0, 0))
    packed = pl.BlockSpec((1,) + parts[0].shape[1:], lambda m, s: (m, 0, 0))
    return pl.pallas_call(
        functools.partial(outer_kernel, len(parts)),
        grid_spec=pltpu.PrefetchScalarGridSpec(
            num_scalar_prefetch=1,
            grid=(modules,),
            in_specs=[packed] * len(parts) + [state, state],
            out_specs=[state, state, packed],
        ),
        out_shape=[
            jax.ShapeDtypeStruct(params.shape, jnp.float32),
            jax.ShapeDtypeStruct(params.shape, jnp.float32),
            jax.ShapeDtypeStruct(parts[0].shape, jnp.bfloat16),
        ],
        compiler_params=pltpu.CompilerParams(vmem_limit_bytes=SMALL_LIMIT),
        cost_estimate=pl.CostEstimate(flops=8 * params.size, bytes_accessed=32 * params.size, transcendentals=0),
        name="outer",
    )(sharing_counts, *parts, params, momentum)


def final_kernel(terms, first_chunk, place_ref, module_ref, weight_ref, step_ref, *refs):
    depth = weight_ref.shape[0]
    grad = refs[0][...].astype(jnp.float32)
    for term in refs[1:terms]:
        grad = grad + term[...].astype(jnp.float32)
    if first_chunk:
        out, rate_out = refs[-2:]
        half = (grad.shape[0] - depth) // 2
        count = BASE * grad[depth : depth + half, :128] + grad[depth + half :, :128]
        rate_out[...] = 0.25 / jnp.sqrt(count)
        rate, grad = rate_out[0:1, 0:1], grad[:depth]
    else:
        rate, out = refs[terms][0:1, 0:1], refs[-1]
    inner = weight_ref[...].astype(jnp.float32) - rate * grad
    rows = step_ref.shape[3]
    left = lax.broadcasted_iota(jnp.int32, (rows, CORES * HALF), 1) < HALF
    for k in range(step_ref.shape[0] // CORES):
        first = step_ref[CORES * k, 0, 0].astype(jnp.float32)
        second = step_ref[CORES * k + 1, 0, 0].astype(jnp.float32)
        top = jnp.where(left, first, pltpu.roll(second, HALF, 1))
        bottom = jnp.where(left, pltpu.roll(first, HALF, 1), second)
        span = slice(k * CORES * HALF, (k + 1) * CORES * HALF)
        out[:rows, span] = (inner[:rows, span] - top).astype(jnp.bfloat16)
        out[rows:, span] = (inner[rows:, span] - bottom).astype(jnp.bfloat16)


def final(place, module_of_path, weights, steps, terms, earlier, chunk, width):
    depth, features = weights.shape
    grid = width // TILE
    base = chunk * grid
    rows, lanes = steps.shape[3:]

    def away(j, s, t):
        return (0, (s[0] // (CORES * Y) + Z_HI - (base + j)) % Z_HI, t[s[0]], 0, 0)

    first = earlier is None
    rate = pl.BlockSpec((8, 128), lambda j, s, t: (0, 0))
    extra = [] if first else [rate, pl.BlockSpec(memory_space=pl.ANY)]
    out = pl.BlockSpec((depth, TILE), lambda j, s, t: (0, base + j))
    result = jax.ShapeDtypeStruct((depth, features), jnp.bfloat16)
    return pl.pallas_call(
        functools.partial(final_kernel, len(terms), first),
        grid_spec=pltpu.PrefetchScalarGridSpec(
            num_scalar_prefetch=2,
            grid=(grid,),
            in_specs=[
                pl.BlockSpec((depth, TILE), lambda j, s, t: (0, base + j)),
                pl.BlockSpec((CORES * Y, 1, 1, rows, lanes), away),
            ]
            + [pl.BlockSpec((terms[0].shape[0], TILE), lambda j, s, t: (0, j))] * len(terms)
            + extra,
            out_specs=[out, rate] if first else out,
        ),
        out_shape=[result, jax.ShapeDtypeStruct((8, 128), jnp.float32)] if first else result,
        input_output_aliases={} if first else {5 + len(terms): 0},
        compiler_params=pltpu.CompilerParams(vmem_limit_bytes=SMALL_LIMIT),
        cost_estimate=pl.CostEstimate(flops=8 * depth * width, bytes_accessed=14 * depth * width, transcendentals=0),
        name="final",
    )(place, module_of_path, weights, steps, *terms, *([] if first else [earlier[1], earlier[0]]))


def after(value, *deps):
    return lax.optimization_barrier((value,) + deps)[0]


def shift(value, way):
    return lax.ppermute(value, "fsdp", way)


def by_offset(s, left, right, far, other, other_left, other_right, other_far):
    pieces = [None] * 8
    pieces[-s % X], pieces[s % X], pieces[2] = left, right, far
    pieces[X], pieces[X + -s % X], pieces[X + s % X], pieces[X + 2] = other, other_left, other_right, other_far
    return pieces[1:]


def gather_first(own):
    up, down, across = ring(1), ring(-1), pair()
    with jax.named_scope("shards"):
        left, right, other = shift(own, up), shift(own, down), shift(own, across)
    begun = (left, right, other)
    with jax.named_scope("shards_on"):
        far = shift(after(left, right, other), up)
        other_right = shift(after(other, left, right), down)
        other_left = shift(after(left, right, other), across)
    with jax.named_scope("shards_last"):
        other_far = shift(after(other_left, far, other_right), up)
    return by_offset(1, left, right, far, other, other_left, other_right, other_far), begun, other_left, other_far


def gather_second(own, other_left_a, other_far_a):
    up, down, across = ring(1), ring(-1), pair()
    with jax.named_scope("late_shards"):
        left = shift(own, down)
        other = shift(after(own, other_left_a), across)
        right = shift(after(own, other_far_a), up)
    with jax.named_scope("late_shards_on"):
        far, other_left, other_right = shift(left, down), shift(left, across), shift(other, up)
    with jax.named_scope("late_shards_last"):
        other_far = shift(other_left, down)
    return by_offset(-1, left, right, far, other, other_left, other_right, other_far), (left, other)


def add(*values):
    total = values[0].astype(jnp.float32)
    for value in values[1:]:
        total = total + value.astype(jnp.float32)
    return total.astype(jnp.bfloat16)


def scatter(blocks, s):
    ahead, back, across = ring(s), ring(-s), pair()
    move = lambda value, way: lax.ppermute(value, "fsdp", way)
    behind, before = -s % X, s % X
    with jax.named_scope("sum_far_other"):
        far_other = move(blocks[X + 2], back)
    with jax.named_scope("sum_near_other"):
        near_other = move(blocks[X + before], ahead)
    with jax.named_scope("sum_far"):
        far = move(after(blocks[2], far_other), back)
    with jax.named_scope("sum_near"):
        near = move(after(blocks[before], near_other), ahead)
    with jax.named_scope("sum_cross_side"):
        cross_side = move(add(blocks[X + behind], far_other), across)
    with jax.named_scope("sum_cross"):
        cross = move(add(blocks[X], near_other), across)
    with jax.named_scope("sum_side"):
        side = move(add(blocks[behind], far, cross_side), back)
    return [blocks[0], near, cross, side], (far_other, near_other)


def per_device(
    inputs,
    targets,
    token_ids,
    path_weights,
    stale_deltas,
    module_params,
    momentum,
    module_of_path,
    sharing_counts,
):
    weights, delta = path_weights[0], stale_deltas[0]
    features = weights.shape[1]
    modules = sharing_counts.shape[0]
    place = jnp.stack([lax.axis_index("path"), lax.axis_index("fsdp")]).astype(jnp.int32)
    width = features // 2

    pieces = [None, None]
    pieces[0], begun, other_left, other_far = gather_first(weights[:, :width])
    normed = norm(place, inputs[0])

    dealt = deal(place, delta)
    dealt = [dealt[0], dealt[1], after(dealt[2], normed), dealt[3]]
    dealt = [dealt[0]] + [lax.ppermute(dealt[k], "path", along_y(k)) for k in range(1, Y)]
    late = after(weights, *begun, *dealt[1:])[:, width:]
    mine, theirs = place_sums(place, module_of_path, dealt, modules, [normed, *begun])
    sums = add(mine, lax.ppermute(theirs, "path", cores()))
    pieces[1], late_begun = gather_second(late, other_left, other_far)
    columns = [[(z * Y + y) * CORES + c for z in range(Z_HI)] for y in range(Y) for c in range(CORES)]
    total = lax.psum_scatter(sums, "path", scatter_dimension=0, axis_index_groups=columns, tiled=True)[0]

    mask = (token_ids[0] != 0).astype(jnp.float32)[:, None]
    blocks = grads(normed, targets[0], mask, weights, pieces[0], 0, width, EXTRA, late_begun)
    new_params, new_momentum, step = outer(
        after(sharing_counts, blocks[0], *pieces[1]),
        [total],
        jnp.swapaxes(module_params, 1, 2),
        jnp.swapaxes(momentum, 1, 2),
    )
    with jax.named_scope("steps_along_z"):
        steps = [step] + [lax.ppermute(step, "path", along_z(k)) for k in range(1, Z_HI)]
    terms, begun = scatter(blocks, 1)
    blocks = grads(normed, targets[0], mask, weights, pieces[1], 1, width, 0)
    planes = [[(z * Y + y) * CORES + c for y in range(Y) for c in range(CORES)] for z in range(Z_HI)]
    steps = after(jnp.stack(steps), blocks[0], *begun)
    steps = lax.all_gather(steps, "path", axis=0, axis_index_groups=planes)
    late_terms, _ = scatter(blocks, -1)
    out = final(place, module_of_path, weights, steps, terms, None, 0, width)
    out = final(place, module_of_path, weights, steps, late_terms, out, 1, width)
    return (out[None], jnp.swapaxes(new_params, 1, 2), jnp.swapaxes(new_momentum, 1, 2))


def solution(mesh):
    return jax.shard_map(
        per_device,
        mesh=mesh,
        in_specs=(
            P("path", "fsdp", None),
            P("path", "fsdp", None),
            P("path", "fsdp"),
            P("path", "fsdp", None),
            P("path", "fsdp", None),
            P(None, "fsdp", "path"),
            P(None, "fsdp", "path"),
            P(),
            P(),
        ),
        out_specs=(P("path", "fsdp", None), P(None, "fsdp", "path"), P(None, "fsdp", "path")),
        check_vma=False,
    )
```
